32 devices in a mesh: req: 4 (over z), tp: 8 (over y, x, core).
Axes of the slice: x: 2, y: 2, z: 4, core: 2. Of those that a mesh axis runs over, the one named last changes fastest.
Arguments:
- queries: bfloat16 [1024, 32, 128], P('req', 'tp'), may hold values from -6 to 6
- key_new: bfloat16 [1024, 8, 128], P('req'), may hold values from -6 to 6
- value_new: bfloat16 [1024, 8, 128], P('req'), may hold values from -6 to 6
- cache_keys: bfloat16 [8, 1024, 8, 128], P('req', 'tp'), may hold values from -6 to 6
- cache_values: bfloat16 [8, 1024, 8, 128], P('req', 'tp'), may hold values from -6 to 6
- context_lengths: int32 [8], P('req'), may hold values from 1 to 1024, 4096 in all
- residual: bfloat16 [1024, 4096], P('req', 'tp'), may hold values from -8 to 8
- out_weight: bfloat16 [4096, 4096], P('tp'), may hold values from -0.125 to 0.125
- norm_gain: bfloat16 [4096], replicated, may hold values from 0.099609375 to 1.8984375
- router: bfloat16 [4096, 4], replicated, may hold values from -0.09375 to 0.09375
- routes: int32 [1024, 2], P('req'), may hold values from 0 to 3, all different within a row; in each aligned block of 256 rows (0 to 255, 256 to 511, ...) at most 256 rows name the same one
- gate_weight: bfloat16 [4, 4096, 14336], P('req', None, 'tp'), may hold values from -0.09375 to 0.09375
- up_weight: bfloat16 [4, 4096, 14336], P('req', None, 'tp'), may hold values from -0.09375 to 0.09375
- down_weight: bfloat16 [4, 14336, 4096], P('req', 'tp'), may hold values from -0.0625 to 0.0625
Outputs:
- layer_out: bfloat16 [1024, 4096], P('req', 'tp')
The draws below stay inside these ranges and needn't reach their ends.
Inputs may be any that keep to these rules, and one draw needn't show every extreme that they name: `routes`: each row names two different experts. Among the rows of one index of req no expert is named by more than 256 rows, and in every draw some expert is named by exactly 256 rows of some index. `context_lengths`: some request uses all 1024 cached positions.
All inputs are finite; a program needn't handle non-finite values. No bound on the sum of `context_lengths` on one device may be relied on, other than what follows from the above.
Results may differ from the reference program's by a relative error of at most 0.015.
Values may be sent and summed in bfloat16 or wider, within the bound.
No kernel may reach another device: no remote copies, remote signals or barrier semaphores. Data moves between devices by JAX's collectives and lax.ppermute only.
A program may use at most 128 MiB of HBM per device.

```python
import math
import jax
import jax.numpy as jnp
import numpy as np
from jax import lax

D = 4096
FF = 14336
H = 32
KVH = 8
HD = 128
TOP = 2
NEW = 128
ROWS_DEV = 256
ROWS = 1024
REQS = 8
L = 1024
EXPERTS = 4
CAP = 256
N_REQ = 4
N_TP = 8


def query_key_pair(key):
    base_key = jax.random.fold_in(key, 23)
    query_seed, keyrow_seed = jax.random.split(base_key, 2)
    query_vals = jnp.clip(jax.random.normal(query_seed, (ROWS, H, HD), jnp.float32), -6.0, 6.0)
    key_vals = jnp.clip(jax.random.normal(keyrow_seed, (ROWS, KVH, HD), jnp.float32), -6.0, 6.0)
    return (query_vals, key_vals)


def draw_queries(key, part):
    return query_key_pair(key)[0].astype(jnp.bfloat16)


def draw_key_new(key, part):
    return query_key_pair(key)[1].astype(jnp.bfloat16)


def draw_residual(key, part):
    base_key = jax.random.fold_in(key, 41)
    value_seed, row_seed, column_seed = jax.random.split(base_key, 3)
    column_ramp = 3.0 ** (jnp.arange(D, dtype=jnp.float32) / D)
    values = jax.random.normal(value_seed, (ROWS, D), jnp.float32)
    row_scale = jnp.exp(jax.random.uniform(row_seed, (ROWS, 1), jnp.float32, math.log(0.3), math.log(3.0)))
    column_scale = column_ramp[None, :] * jnp.exp(jax.random.uniform(column_seed, (1, D), jnp.float32, -0.6, 0.6)) / 1.7
    values = values * column_scale * row_scale
    return jnp.clip(values, -8.0, 8.0).astype(jnp.bfloat16)


def spiked(drawn, key, source, target, blocks, factor):
    def block_of(dim):
        return (jnp.arange(drawn.shape[dim]) // (drawn.shape[dim] // blocks)).reshape((-1,) + (1,) * (drawn.ndim - 1 - dim))

    one_side = jax.random.permutation(key, blocks)[block_of(target)]
    other_side = (block_of(target) + blocks // 2) % blocks
    return jnp.where((block_of(source) == one_side) | (block_of(source) == other_side), factor * drawn, drawn)


def levels(own_key, shape, shards, least, high):
    gain, own = 1.0, jax.random.fold_in(own_key, 6)
    for axis_at, blocks in shards:
        draws = jnp.exp(jax.random.uniform(jax.random.fold_in(own, axis_at), (blocks,), jnp.float32, least / len(shards), high / len(shards)))
        gain = gain * jnp.repeat(draws, shape[axis_at] // blocks).reshape([-1 if axis == axis_at else 1 for axis in range(len(shape))])
    return gain


def split_up(amount, total, bound, slope):
    loads = [(1 << 20) // math.isqrt(grade ** slope) + 1 for grade in range(2, amount + 1)]
    surplus, given = total - bound - (amount - 1), [1] * (amount - 1)
    while surplus > 0:
        candidates = [i for i in range(amount - 1) if given[i] < bound]
        pool, budget = sum([loads[i] for i in candidates]), surplus
        for i in candidates:
            extra = min(bound - given[i], max(1, budget * loads[i] // pool), surplus)
            given[i] = given[i] + extra
            surplus = surplus - extra
    return np.array([bound] + given)


def uneven_parts(key, amount, total, most, skew):
    if amount == 2:
        one = jax.random.randint(key, (), max(1, total - most), min(most, total - 1) + 1)
        return jnp.stack([one, total - one])
    sizes = jnp.asarray(split_up(amount, total, most, skew), jnp.int32)
    couples = (amount - 1) // 2
    source_of, receiver = sizes[1:1 + 2 * couples:2], sizes[2:2 + 2 * couples:2]
    room = jnp.minimum(source_of - 1, most - receiver)
    passed = jax.random.randint(jax.random.fold_in(key, 1), (couples,), 0, 1 << 20) % (room + 1)
    sizes = sizes.at[1:1 + 2 * couples:2].set(source_of - passed).at[2:2 + 2 * couples:2].set(receiver + passed)
    return sizes[jax.random.permutation(jax.random.fold_in(key, 2), amount)]


def assign_block(own_key, own, number, rows, amount, top, reach, lean):
    sequence = jax.random.permutation(own_key, amount)
    heavy_load, common = load_shares(amount, rows * top, reach, lean, True), load_shares(amount, rows * top, reach, lean, False)
    places = jnp.arange(amount)

    def named(lengths, rotation):
        used = int((lengths > 0).sum())
        fixed = max(1, used // 4)
        moved = fixed + (places - fixed + rotation * (used - fixed)) % max(1, amount - fixed)
        return jnp.zeros((amount,), jnp.int32).at[sequence[jnp.where(places < fixed, places, moved)]].set(jnp.asarray(lengths, jnp.int32))

    lengths = jnp.where(number % 4 == 0, named(heavy_load, number // 4), named(common, number - number // 4 - 1))
    mixed = jax.random.permutation(jax.random.fold_in(own, 3), amount)
    source_of, taker = mixed[0:amount // 2 * 2:2], mixed[1:amount // 2 * 2:2]
    room = jnp.minimum(lengths[source_of] - 1, reach - lengths[taker]) // 2
    room = jnp.where((source_of == sequence[0]) | (taker == sequence[0]) | (lengths[taker] == 0), 0, jnp.maximum(room, 0))
    moved = jax.random.randint(jax.random.fold_in(own, 4), (amount // 2,), 0, 1 << 20) % (room + 1)
    lengths = lengths.at[source_of].add(-moved).at[taker].add(moved)
    labels = jnp.searchsorted(jnp.cumsum(lengths), jnp.arange(rows * top), side="right").astype(jnp.int32)
    table = labels.reshape(top, rows).T
    table = table[jax.random.permutation(jax.random.fold_in(own, 1), rows)]
    rotation = jax.random.randint(jax.random.fold_in(own, 2), (rows, 1), 0, top)
    return jnp.take_along_axis(table, (jnp.arange(top)[None, :] + rotation) % top, axis=1)


def load_shares(amount, total, reach, lean, full):
    portions = [(1 << 20) // math.isqrt(standing ** lean) + 1 for standing in range(1, amount + 1)]
    largest = reach if full else min(reach, max(-(-total // amount), total * portions[0] // sum(portions)))
    least = 1 if total - largest >= amount - 1 else 0
    holding, rest = [largest] + [least] * (amount - 1), total - largest - least * (amount - 1)
    while rest > 0:
        candidates = [i for i in range(1, amount) if holding[i] < largest] or [i for i in range(1, amount) if holding[i] < reach]
        mass, budget = sum([portions[i] for i in candidates]), rest
        for i in candidates:
            addition = min(reach - holding[i], max(1, budget * portions[i] // mass), rest)
            holding[i] = holding[i] + addition
            rest = rest - addition
    return np.array(holding)


def centred(rng, dims, scale, limit, cuts=(), kind=jnp.bfloat16):
    result = jax.random.normal(rng, dims, jnp.float32) * scale
    if len(cuts) > 0:
        result = levels(rng, dims, cuts, -0.22, 0.18) * result
    return jnp.clip(result, min=-limit, max=limit).astype(kind)


def heavy_noise(key, dims, deviation, most, shards, heavy, kind=jnp.bfloat16):
    drawn = deviation * jax.random.normal(key, dims, jnp.float32)
    if shards:
        drawn = drawn * levels(key, dims, shards, -0.22, 0.18)
    return jnp.clip(spiked(drawn, jax.random.fold_in(key, 3), *heavy), -most, most).astype(kind)


def setup_inputs(seed: int = 0) -> dict:
    streams_of = jax.random.split(jax.random.key(seed), 15)
    queries = draw_queries(jax.random.fold_in(streams_of[14], 71), 0)
    key_new = draw_key_new(jax.random.fold_in(streams_of[14], 71), 0)
    value_new = centred(streams_of[2], (ROWS, KVH, HD), 1.0, 6.0, ((0, 4),))
    cache_keys = centred(streams_of[3], (REQS, L, KVH, HD), 1.0, 6.0, ((0, 4), (1, 8)))
    cache_values = centred(streams_of[4], (REQS, L, KVH, HD), 1.0, 6.0, ((0, 4), (1, 8)))
    context_lengths = uneven_parts(streams_of[5], REQS, REQS * L // 2, L, 2).astype(jnp.int32)
    residual = draw_residual(jax.random.fold_in(streams_of[14], 71), 0)
    out_weight = heavy_noise(streams_of[7], (H * HD, D), (H * HD) ** -0.5, 0.125, ((0, 8),), (0, 1, 8, 2.0))
    norm_gain = jnp.clip(1.0 + 0.18 * jax.random.normal(streams_of[8], (D,), jnp.float32), 0.099609375, 1.8984375).astype(jnp.bfloat16)
    router = centred(streams_of[9], (D, EXPERTS), D ** -0.5, 0.09375)
    routes_keys = jax.random.split(jax.random.fold_in(streams_of[10], 1), ROWS // ROWS_DEV)
    routes_turns = jax.random.permutation(jax.random.fold_in(streams_of[10], 3), ROWS // ROWS_DEV)
    routes = jax.vmap(lambda own, number: assign_block(jax.random.fold_in(streams_of[10], 2), own, number, ROWS_DEV, EXPERTS, TOP, CAP, 2))(routes_keys, routes_turns).reshape((ROWS, TOP))
    gate_weight = centred(streams_of[11], (EXPERTS, D, FF), D ** -0.5, 0.09375, ((0, 4), (2, 8)))
    up_weight = centred(streams_of[12], (EXPERTS, D, FF), D ** -0.5, 0.09375, ((0, 4), (2, 8)))
    down_weight = heavy_noise(streams_of[13], (EXPERTS, FF, D), FF ** -0.5, 0.0625, ((0, 4), (1, 8)), (1, 2, 8, 2.0))
    return {"queries": queries, "key_new": key_new, "value_new": value_new, "cache_keys": cache_keys, "cache_values": cache_values, "context_lengths": context_lengths, "residual": residual, "out_weight": out_weight, "norm_gain": norm_gain, "router": router, "routes": routes, "gate_weight": gate_weight, "up_weight": up_weight, "down_weight": down_weight}


norm_eps = 1e-05
masked_score = -1e+30

def round_trip(values):
    return lax.optimization_barrier(values.astype(jnp.bfloat16)).astype(jnp.float32)

def slot_places(route_block, experts, capacity):
    chosen = route_block.reshape(-1).astype(jnp.int32)
    indicator = (chosen[:, None] == jnp.arange(experts, dtype=jnp.int32)[None, :]).astype(jnp.int32)
    earlier = (jnp.cumsum(indicator, axis=0).astype(jnp.int32) - indicator).astype(jnp.int32)
    within = lax.optimization_barrier(jnp.sum(earlier * indicator, axis=1)).astype(jnp.int32)
    return (chosen * capacity + within).astype(jnp.int32)

def pick_logit(logits, column, experts):
    matches = column[:, None] == jnp.arange(experts, dtype=jnp.int32)[None, :]
    return lax.optimization_barrier(jnp.sum(jnp.where(matches, logits, 0.0), axis=1))

def attend_request(query_block, cached_keys, cached_values, new_keys, new_values, length):
    grouping = H // KVH
    key_all = jnp.concatenate([cached_keys, new_keys], axis=0).astype(jnp.float32)
    value_all = jnp.concatenate([cached_values, new_values], axis=0).astype(jnp.float32)
    query_all = query_block.astype(jnp.float32).reshape(NEW, KVH, grouping, HD)
    scores = jnp.einsum('nkgd,lkd->nkgl', query_all, key_all) * HD ** (-0.5)
    cache_allowed = jnp.arange(L, dtype=jnp.int32)[None, :] < length
    new_steps = jnp.arange(NEW, dtype=jnp.int32)
    new_allowed = new_steps[None, :] <= new_steps[:, None]
    allowed = jnp.concatenate([jnp.broadcast_to(cache_allowed, (NEW, L)), new_allowed], axis=1)[:, None, None, :]
    scores = jnp.where(allowed, scores, masked_score)
    highest = lax.optimization_barrier(jnp.max(scores, axis=-1, keepdims=True))
    weights = jnp.where(allowed, jnp.exp(scores - highest), 0.0)
    denominator = lax.optimization_barrier(jnp.sum(weights, axis=-1, keepdims=True))
    mixture = jnp.einsum('nkgl,lkd->nkgd', round_trip(weights), value_all) / denominator
    return mixture.reshape(NEW, H * HD).astype(jnp.bfloat16)

def reference(queries, key_new, value_new, cache_keys, cache_values, context_lengths, residual, out_weight, norm_gain, router, routes, gate_weight, up_weight, down_weight):
    query_blocks = queries.reshape(REQS, NEW, H, HD)
    key_blocks = key_new.reshape(REQS, NEW, KVH, HD)
    value_blocks = value_new.reshape(REQS, NEW, KVH, HD)
    attention = lax.map(lambda packed: attend_request(*packed), (query_blocks, cache_keys, cache_values, key_blocks, value_blocks, context_lengths))
    attention = attention.reshape(ROWS, H * HD)
    column_width = H * HD // N_TP

    def add_heads(group_index, running):
        offset = group_index * column_width
        partial_value = jnp.dot(lax.dynamic_slice_in_dim(attention, offset, column_width, 1), lax.dynamic_slice_in_dim(out_weight, offset, column_width, 0), preferred_element_type=jnp.float32)
        return running + round_trip(partial_value)
    attention_sum = lax.fori_loop(jnp.int32(0), jnp.int32(N_TP), add_heads, jnp.zeros((ROWS, D), jnp.float32))
    hidden = (residual.astype(jnp.float32) + attention_sum).astype(jnp.bfloat16)
    hidden_float = hidden.astype(jnp.float32)
    inverse_rms = lax.rsqrt(lax.optimization_barrier(jnp.mean(hidden_float * hidden_float, axis=1, keepdims=True)) + norm_eps)
    normed_float = hidden_float * inverse_rms * norm_gain.astype(jnp.float32)[None, :]
    logits = jnp.dot(normed_float, router.astype(jnp.float32), precision=lax.Precision.HIGHEST)
    logit_first = pick_logit(logits, routes[:, 0], EXPERTS)
    logit_second = pick_logit(logits, routes[:, 1], EXPERTS)
    weight_first = 1.0 / (1.0 + jnp.exp(logit_second - logit_first))
    weight_second = 1.0 / (1.0 + jnp.exp(logit_first - logit_second))
    normed = normed_float.astype(jnp.bfloat16)
    route_grid = routes.reshape(N_REQ, ROWS_DEV, TOP)
    places = jax.vmap(lambda route_block: slot_places(route_block, EXPERTS, CAP))(route_grid)
    pair_rows = jnp.repeat(jnp.arange(ROWS_DEV, dtype=jnp.int32), TOP)
    sources = jax.vmap(lambda slot_spots: jnp.full((EXPERTS * CAP,), ROWS_DEV, jnp.int32).at[slot_spots].set(pair_rows))(places)
    root = (jnp.arange(N_REQ, dtype=jnp.int32) * ROWS_DEV)[:, None]
    global_rows = jnp.where(sources < ROWS_DEV, sources + root, ROWS).astype(jnp.int32)
    expert_rows = jnp.transpose(global_rows.reshape(N_REQ, EXPERTS, CAP), (1, 0, 2)).reshape(EXPERTS, N_REQ * CAP)
    padded = jnp.concatenate([normed, jnp.zeros((1, D), jnp.bfloat16)], axis=0)
    unit_width = FF // N_TP

    def run_expert(packed):
        row_index, gate_matrix, up_matrix, down_matrix = packed
        inputs = padded[row_index]
        gate_sums = jnp.dot(inputs, gate_matrix, preferred_element_type=jnp.float32)
        up_sums = jnp.dot(inputs, up_matrix, preferred_element_type=jnp.float32)
        activated = (jax.nn.silu(gate_sums) * up_sums).astype(jnp.bfloat16)

        def add_units(group_index, running):
            offset = group_index * unit_width
            partial_value = jnp.dot(lax.dynamic_slice_in_dim(activated, offset, unit_width, 1), lax.dynamic_slice_in_dim(down_matrix, offset, unit_width, 0), preferred_element_type=jnp.float32)
            return running + round_trip(partial_value)
        summed = lax.fori_loop(jnp.int32(0), jnp.int32(N_TP), add_units, jnp.zeros((N_REQ * CAP, D), jnp.float32))
        return summed.astype(jnp.bfloat16)
    expert_out = lax.map(run_expert, (expert_rows, gate_weight, up_weight, down_weight)).reshape(EXPERTS * N_REQ * CAP, D)
    slot_spots = places.reshape(ROWS, TOP)
    group_of_row = (jnp.arange(ROWS, dtype=jnp.int32) // ROWS_DEV)[:, None]
    flat_index = (slot_spots // CAP * (N_REQ * CAP) + group_of_row * CAP + slot_spots % CAP).astype(jnp.int32)
    first_out = expert_out[flat_index[:, 0]].astype(jnp.float32)
    second_out = expert_out[flat_index[:, 1]].astype(jnp.float32)
    combined = hidden_float + weight_first[:, None] * first_out + weight_second[:, None] * second_out
    return combined.astype(jnp.bfloat16)
```

```python
import functools
import jax
import jax.numpy as jnp
from jax import lax
from jax.experimental import pallas as pl
from jax.experimental.pallas import tpu as pltpu
from jax.sharding import PartitionSpec as P

norm_eps = 1e-05
masked_score = -1e30
bf16 = jnp.bfloat16
f32 = jnp.float32
MIB = 1 << 20
unit_block = 512


def xor_swap(x, axis, mask):
    size = lax.axis_size(axis)
    return lax.ppermute(x, axis, [(i, i ^ mask) for i in range(size)])


def attend_kernel(devices, groups, scaling, lengths_ref, rank_ref, *refs):
    cached_ref, q_ref, kn_ref, vn_ref, ow_hbm, like_ref, other_ref, ow_ref, semaphore = refs
    fetch = pltpu.make_async_copy(ow_hbm, ow_ref, semaphore)

    @pl.when(pl.program_id(0) == 0)
    def _():
        fetch.start()

    rank = rank_ref[0]
    length = lengths_ref[pl.program_id(0)]
    key_heads, new_rows, width = kn_ref.shape
    span = cached_ref.shape[4]
    columns = like_ref.shape[2]
    cached = devices * span
    column = lax.broadcasted_iota(jnp.int32, (new_rows, cached), 1)
    far_bias = jnp.where(column < length, 0.0, masked_score)
    row = lax.broadcasted_iota(jnp.int32, (new_rows, new_rows), 0)
    step = lax.broadcasted_iota(jnp.int32, (new_rows, new_rows), 1)
    near_bias = jnp.where(step <= row, 0.0, masked_score)
    bias = jnp.concatenate([far_bias, near_bias], axis=1)
    outs = []
    for head in range(key_heads):
        keys = jnp.concatenate([cached_ref[d, head, 0, 0] for d in range(devices)] + [kn_ref[head]], axis=0)
        values = jnp.concatenate([cached_ref[d, head, 1, 0] for d in range(devices)] + [vn_ref[head]], axis=0)
        for g in range(groups):
            q = q_ref[head * groups + g]
            scores = (
                lax.dot_general(q, keys, (((1,), (1,)), ((), ())), preferred_element_type=f32)
                * scaling
            )
            scores = jnp.where(bias < 0.0, masked_score, scores)
            highest = jnp.max(scores, axis=1, keepdims=True)
            weights = jnp.exp(scores - highest)
            total = jnp.sum(weights, axis=1, keepdims=True)
            mixed = jnp.dot(weights.astype(bf16), values, preferred_element_type=f32)
            outs.append((mixed / total).astype(bf16))
    attention = jnp.concatenate(outs, axis=1)

    @pl.when(pl.program_id(0) == 0)
    def _():
        fetch.wait()

    for target, parity in ((like_ref, 0), (other_ref, 1)):
        for i in range(devices // 2):
            first = pl.multiple_of((rank ^ (2 * i + parity)) * columns, columns)
            term = jnp.dot(attention, ow_ref[:, pl.ds(first, columns)], preferred_element_type=f32)
            target[i] = term.astype(bf16)


def attend(lengths, rank, cached, q, kn, vn, out_weight, scaling):
    devices, key_heads, _, requests, span, width = cached.shape
    heads, rows, _ = q.shape
    new_rows = rows // requests
    model = out_weight.shape[1]
    columns = model // devices
    cached_spec = pl.BlockSpec(
        (devices, key_heads, 2, 1, span, width), lambda r, *_: (0, 0, 0, r, 0, 0)
    )
    near_spec = pl.BlockSpec((key_heads, new_rows, width), lambda r, *_: (0, r, 0))
    out_spec = pl.BlockSpec((devices // 2, new_rows, columns), lambda r, *_: (0, r, 0))
    out_type = jax.ShapeDtypeStruct((devices // 2, rows, columns), bf16)
    flops = 4 * rows * heads * width * (devices * span + new_rows) + 2 * rows * heads * width * model
    return pl.pallas_call(
        functools.partial(attend_kernel, devices, heads // key_heads, scaling),
        grid_spec=pltpu.PrefetchScalarGridSpec(
            num_scalar_prefetch=2,
            grid=(requests,),
            in_specs=[
                cached_spec,
                pl.BlockSpec((heads, new_rows, width), lambda r, *_: (0, r, 0)),
                near_spec,
                near_spec,
                pl.BlockSpec(memory_space=pl.ANY),
            ],
            out_specs=[out_spec, out_spec],
            scratch_shapes=[pltpu.VMEM(out_weight.shape, bf16), pltpu.SemaphoreType.DMA],
        ),
        out_shape=[out_type, out_type],
        compiler_params=pltpu.CompilerParams(vmem_limit_bytes=58 * MIB),
        cost_estimate=pl.CostEstimate(
            flops=flops, bytes_accessed=8 * MIB, transcendentals=rows * heads * devices * span
        ),
        name="attend",
    )(lengths, rank, cached, q, kn, vn, out_weight)


def blocks_of(size, block):
    return [(first, min(block, size - first)) for first in range(0, size, block)]


def units_kernel(devices, experts, scalars_ref, *refs):
    like_ref, other_ref, gain_ref, router_ref, routes_ref = refs[:5]
    gate_hbm, up_hbm, down_hbm, active_ref, weight_ref, odd_ref, down_ref = refs[5:12]
    normed_ref, gate_ref, up_ref, down_odd_ref, semaphores = refs[12:]
    spans = blocks_of(active_ref.shape[1], unit_block)
    count = len(spans)

    def fetch(n):
        first, size = spans[n]
        copies = [
            pltpu.make_async_copy(
                source.at[:, pl.ds(first, size)],
                target.at[n % 2, :, pl.ds(0, size)],
                semaphores.at[2 * n + i],
            )
            for i, (source, target) in enumerate(((gate_hbm, gate_ref), (up_hbm, up_ref)))
        ]
        for copy in copies:
            copy.start()
        return copies

    rank, expert = scalars_ref[0], scalars_ref[1]
    half, rows, columns = like_ref.shape
    model = devices * columns

    def fetch_down(n):
        parity, i = (1, n) if n < half else (0, n - half)
        first = pl.multiple_of((rank ^ (2 * i + parity)) * columns, columns)
        target = (down_odd_ref if parity else down_ref).at[i]
        copy = pltpu.make_async_copy(down_hbm.at[:, pl.ds(first, columns)], target, semaphores.at[2 * count + n])
        copy.start()
        return copy

    fetched, downs = [fetch(0)], []

    pieces = []
    for ref, parity in ((like_ref, 0), (other_ref, 1)):
        pieces += [(ref, i, rank ^ (2 * i + parity)) for i in range(devices // 2)]
    squares = jnp.zeros((rows, 1), f32)
    raw = jnp.zeros((rows, router_ref.shape[1]), f32)
    for ref, i, device in pieces:
        first = pl.multiple_of(device * columns, columns)
        value = ref[i].astype(f32)
        squares += jnp.sum(value * value, axis=1, keepdims=True)
        raw += jnp.dot(ref[i], router_ref[pl.ds(first, columns), :], preferred_element_type=f32)
    inverse = lax.rsqrt(squares / model + norm_eps)
    for ref, i, device in pieces:
        first = pl.multiple_of(device * columns, columns)
        value = ref[i].astype(f32) * inverse * gain_ref[device]
        normed_ref[:, pl.ds(first, columns)] = value.astype(bf16)
    logits = raw * inverse
    routes = routes_ref[...]
    one, two = routes[:, 0:1], routes[:, 1:2]
    lane = lax.broadcasted_iota(jnp.int32, raw.shape, 1)
    lane = jnp.where(lane < experts, lane, lane - experts)
    own_logit = jnp.sum(jnp.where(lane == expert, logits, 0.0), axis=1, keepdims=True)
    other_logit = jnp.sum(jnp.where(lane == one + two - expert, logits, 0.0), axis=1, keepdims=True)
    named = (one == expert) | (two == expert)
    weight = jnp.where(named, 1.0 / (1.0 + jnp.exp(other_logit - own_logit)), 0.0)
    weight_ref[...] = jnp.broadcast_to(weight, weight_ref.shape)

    for n, (first, size) in enumerate(spans):
        if n + 1 < count:
            fetched.append(fetch(n + 1))
        downs += [fetch_down(m) for m in range(len(downs), 2 * half * (n + 1) // (count + 1))]
        for copy in fetched[n]:
            copy.wait()
        block = n % 2, slice(None), pl.ds(0, size)
        gate = jnp.dot(normed_ref[...], gate_ref[block], preferred_element_type=f32)
        up = jnp.dot(normed_ref[...], up_ref[block], preferred_element_type=f32)
        active_ref[:, pl.ds(first, size)] = (gate / (1.0 + jnp.exp(-gate)) * up).astype(bf16)
    downs += [fetch_down(m) for m in range(len(downs), 2 * half)]
    for i in range(half):
        downs[i].wait()
        total = jnp.dot(active_ref[...], down_odd_ref[i], preferred_element_type=f32)
        odd_ref[i] = (total * weight_ref[:, 0:1]).astype(bf16)
    for copy in downs[half:]:
        copy.wait()


def run_units(experts, scalars, like, other, gain, router, routes, weights):
    half, rows, columns = like.shape
    model, units = weights[0].shape
    in_vmem = pl.BlockSpec(memory_space=pltpu.VMEM)
    in_hbm = pl.BlockSpec(memory_space=pl.ANY)
    out_shape = [jax.ShapeDtypeStruct((rows, units), bf16), jax.ShapeDtypeStruct((rows, 128), f32)]
    out_shape.append(jax.ShapeDtypeStruct((half, rows, columns), bf16))
    out_shape.append(pltpu.VMEM((half, units, columns), bf16))
    block = min(unit_block, units)
    return pl.pallas_call(
        functools.partial(units_kernel, 2 * half, experts),
        in_specs=[pl.BlockSpec(memory_space=pltpu.SMEM)] + [in_vmem] * 5 + [in_hbm] * len(weights),
        out_specs=[in_vmem] * len(out_shape),
        out_shape=out_shape,
        scratch_shapes=[
            pltpu.VMEM((rows, model), bf16),
            pltpu.VMEM((2, model, block), bf16),
            pltpu.VMEM((2, model, block), bf16),
            pltpu.VMEM((half, units, columns), bf16),
            pltpu.SemaphoreType.DMA((2 * len(blocks_of(units, block)) + 2 * half,)),
        ],
        compiler_params=pltpu.CompilerParams(vmem_limit_bytes=38 * MIB),
        cost_estimate=pl.CostEstimate(
            flops=4 * rows * model * units, bytes_accessed=6 * model * units, transcendentals=rows * units
        ),
        name="units",
    )(scalars, like, other, gain, router, routes, *weights)


def down_kernel(active_ref, weight_ref, down_ref, out_ref):
    for i in range(out_ref.shape[0]):
        total = jnp.dot(active_ref[...], down_ref[i], preferred_element_type=f32)
        out_ref[i] = (total * weight_ref[:, 0:1]).astype(bf16)


def run_down(active, weight, down):
    rows = active.shape[0]
    half, units, columns = down.shape
    in_vmem = pl.BlockSpec(memory_space=pltpu.VMEM)
    return pl.pallas_call(
        down_kernel,
        in_specs=[in_vmem] * 3,
        out_specs=in_vmem,
        out_shape=jax.ShapeDtypeStruct((half, rows, columns), bf16),
        compiler_params=pltpu.CompilerParams(vmem_limit_bytes=8 * MIB),
        cost_estimate=pl.CostEstimate(
            flops=2 * rows * down.size, bytes_accessed=2 * down.size, transcendentals=0
        ),
        name="down",
    )(active, weight, down)


def fence(*values):
    return lax.optimization_barrier(values)


def between_chips(piece):
    devices = lax.axis_size("tp")
    return [piece] + [xor_swap(piece, "tp", j) for j in range(2, devices, 2)]


def core_sums(like, arrived):
    return [
        (like[i].astype(f32) + arrived[i].astype(f32)).astype(bf16) for i in range(like.shape[0])
    ]


def scatter_chips(sums):
    return [sums[0]] + [xor_swap(x, "tp", 2 * i) for i, x in enumerate(sums) if i > 0]


def add_up(parts):
    total = parts[0].astype(f32)
    for x in parts[1:]:
        total += x.astype(f32)
    return total


def per_device(
    queries,
    key_new,
    value_new,
    cache_keys,
    cache_values,
    context_lengths,
    residual,
    out_weight,
    norm_gain,
    router,
    routes,
    gate_weight,
    up_weight,
    down_weight,
):
    devices = lax.axis_size("tp")
    planes = lax.axis_size("req")
    rank = lax.axis_index("tp")
    plane = lax.axis_index("req")
    heads, width = queries.shape[1], queries.shape[2]
    key_heads = cache_keys.shape[2]
    grouping = heads * devices // key_heads
    own_keys = max(1, heads // grouping)
    model = out_weight.shape[1]
    columns = model // devices

    cache = jnp.stack([cache_keys, cache_values]).transpose(3, 0, 1, 2, 4)
    if own_keys * devices != key_heads:
        cache = jnp.repeat(cache, own_keys * devices // key_heads, axis=0)
    cache = cache.reshape(devices, own_keys, *cache.shape[1:])
    cached = lax.all_to_all(cache, "tp", split_axis=0, concat_axis=0, tiled=True)
    first_key = rank * heads // grouping
    kn = lax.dynamic_slice_in_dim(key_new, first_key, own_keys, 1).transpose(1, 0, 2)
    vn = lax.dynamic_slice_in_dim(value_new, first_key, own_keys, 1).transpose(1, 0, 2)
    q = queries.transpose(1, 0, 2)
    gain = norm_gain.astype(f32)
    routing = gain[:, None] * router.astype(f32)
    high = routing.astype(bf16)
    low = (routing - high.astype(f32)).astype(bf16)
    routing = jnp.concatenate([high, low], axis=1)
    routing = jnp.pad(routing, ((0, 0), (0, -routing.shape[1] % 128)))
    gain = gain.reshape(devices, 1, columns)
    scalars = jnp.stack([rank, plane]).astype(jnp.int32)
    cached, routing, gain, scalars, q, kn, vn = fence(cached, routing, gain, scalars, q, kn, vn)

    like, other = attend(
        context_lengths, scalars[:1], cached, q, kn, vn, out_weight, width**-0.5
    )
    sums = core_sums(like, xor_swap(other, "tp", 1))
    sums, own_routes = fence(sums, routes)
    parts = scatter_chips(sums)
    chunk_routes = [own_routes] + [xor_swap(own_routes, "req", k) for k in range(1, planes)]
    parts, chunk_routes = fence(parts, chunk_routes)
    hidden = (residual.astype(f32) + add_up(parts)).astype(bf16)

    groups = [[0]] + [list(range(k, min(k + 2, planes))) for k in range(1, planes, 2)]
    half = devices // 2
    span = hidden.shape[0]
    weights = [gate_weight[0], up_weight[0], down_weight[0]]

    def joined(arrays, group):
        return arrays[group[0]] if len(group) == 1 else jnp.concatenate([arrays[k] for k in group], axis=0)

    def rows_of(near):
        rows = jnp.stack(near)
        return rows, xor_swap(rows, "tp", 1)

    near = between_chips(hidden)
    pieces = {k: xor_swap(hidden, "req", k) for k in range(1, min(planes, 3))}
    near, pieces, own = fence(near, pieces, hidden)
    pieces |= {k: xor_swap(own, "req", k) for k in range(3, planes)}
    like, other = rows_of(near)
    spread, back = {}, {}

    def send_back():
        for at in list(spread):
            total = add_up(spread.pop(at))
            for i, k in enumerate(groups[at]):
                part = total[i * span : (i + 1) * span]
                back[k] = xor_swap(part.astype(bf16), "req", k) if k else part

    for at, group in enumerate(groups):
        following = groups[at + 1] if at + 1 < len(groups) else None
        near = between_chips(joined(pieces, following)) if following else []
        active, weight, odd, down = run_units(
            planes, scalars, like, other, gain, routing, joined(chunk_routes, group), weights
        )
        near, spread, pieces, active, weight, odd, down = fence(
            near, spread, pieces, active, weight, odd, down
        )
        if following:
            like, other = rows_of(near)
        send_back()
        arrived = xor_swap(odd, "tp", 1)
        even = run_down(active, weight, down)
        even, arrived, other, pieces = fence(even, arrived, other, pieces)
        spread[at] = scatter_chips(core_sums(even, arrived))
    send_back()
    total = hidden.astype(f32)
    for k in range(planes):
        total += back[k].astype(f32)
    return total.astype(bf16)


def solution(mesh):
    placed = (
        P("req", "tp", None),
        P("req", None, None),
        P("req", None, None),
        P("req", "tp", None, None),
        P("req", "tp", None, None),
        P("req"),
        P("req", "tp"),
        P("tp", None),
        P(),
        P(),
        P("req", None),
        P("req", None, "tp"),
        P("req", None, "tp"),
        P("req", "tp", None),
    )
    return jax.shard_map(
        per_device, mesh=mesh, in_specs=placed, out_specs=P("req", "tp"), check_vma=False
    )
```

```python
import functools
import jax
import jax.numpy as jnp
from jax import lax
from jax.experimental import pallas as pl
from jax.experimental.pallas import tpu as pltpu
from jax.sharding import PartitionSpec as P

norm_eps = 1e-05
masked_score = -1e30
bf16 = jnp.bfloat16
f32 = jnp.float32
MIB = 1 << 20
unit_block = 512


def xor_swap(x, axis, mask):
    size = lax.axis_size(axis)
    return lax.ppermute(x, axis, [(i, i ^ mask) for i in range(size)])


def attend_kernel(devices, groups, scaling, lengths_ref, rank_ref, *refs):
    pieces, (q_ref, kn_ref, vn_ref, ow_ref, like_ref, other_ref) = refs[:devices], refs[devices:]
    rank = rank_ref[0]
    length = lengths_ref[pl.program_id(0)]
    key_heads, new_rows, width = kn_ref.shape
    span = pieces[0].shape[3]
    columns = like_ref.shape[2]
    cached = devices * span
    column = lax.broadcasted_iota(jnp.int32, (new_rows, cached), 1)
    place = (rank ^ (column // span)) * span + column % span
    far_bias = jnp.where(place < length, 0.0, masked_score)
    row = lax.broadcasted_iota(jnp.int32, (new_rows, new_rows), 0)
    step = lax.broadcasted_iota(jnp.int32, (new_rows, new_rows), 1)
    near_bias = jnp.where(step <= row, 0.0, masked_score)
    bias = jnp.concatenate([far_bias, near_bias], axis=1)
    outs = []
    for head in range(key_heads):
        keys = jnp.concatenate([p[0, head, 0] for p in pieces] + [kn_ref[head]], axis=0)
        values = jnp.concatenate([p[1, head, 0] for p in pieces] + [vn_ref[head]], axis=0)
        for g in range(groups):
            q = q_ref[head * groups + g]
            scores = (
                lax.dot_general(q, keys, (((1,), (1,)), ((), ())), preferred_element_type=f32)
                * scaling
            )
            scores = jnp.where(bias < 0.0, masked_score, scores)
            highest = jnp.max(scores, axis=1, keepdims=True)
            weights = jnp.exp(scores - highest)
            total = jnp.sum(weights, axis=1, keepdims=True)
            mixed = jnp.dot(weights.astype(bf16), values, preferred_element_type=f32)
            outs.append((mixed / total).astype(bf16))
    attention = jnp.concatenate(outs, axis=1)
    for target, parity in ((like_ref, 0), (other_ref, 1)):
        for i in range(devices // 2):
            first = pl.multiple_of((rank ^ (2 * i + parity)) * columns, columns)
            term = jnp.dot(attention, ow_ref[:, pl.ds(first, columns)], preferred_element_type=f32)
            target[i] = term.astype(bf16)


def attend(lengths, rank, cached, q, kn, vn, out_weight, scaling):
    devices = len(cached)
    _, key_heads, requests, span, width = cached[0].shape
    heads, rows, _ = q.shape
    new_rows = rows // requests
    model = out_weight.shape[1]
    columns = model // devices
    cached_spec = pl.BlockSpec((2, key_heads, 1, span, width), lambda r, *_: (0, 0, r, 0, 0))
    near_spec = pl.BlockSpec((key_heads, new_rows, width), lambda r, *_: (0, r, 0))
    out_spec = pl.BlockSpec((devices // 2, new_rows, columns), lambda r, *_: (0, r, 0))
    out_type = jax.ShapeDtypeStruct((devices // 2, rows, columns), bf16)
    flops = 4 * rows * heads * width * (devices * span + new_rows) + 2 * rows * heads * width * model
    return pl.pallas_call(
        functools.partial(attend_kernel, devices, heads // key_heads, scaling),
        grid_spec=pltpu.PrefetchScalarGridSpec(
            num_scalar_prefetch=2,
            grid=(requests,),
            in_specs=[cached_spec] * devices
            + [
                pl.BlockSpec((heads, new_rows, width), lambda r, *_: (0, r, 0)),
                near_spec,
                near_spec,
                pl.BlockSpec(memory_space=pltpu.VMEM),
            ],
            out_specs=[out_spec, out_spec],
        ),
        out_shape=[out_type, out_type],
        compiler_params=pltpu.CompilerParams(vmem_limit_bytes=24 * MIB),
        cost_estimate=pl.CostEstimate(
            flops=flops, bytes_accessed=8 * MIB, transcendentals=rows * heads * devices * span
        ),
        name="attend",
    )(lengths, rank, *cached, q, kn, vn, out_weight)


def hold_kernel(source_ref, target_ref, semaphores):
    parts = semaphores.shape[0]
    rows = source_ref.shape[0] // parts
    copies = [
        pltpu.make_async_copy(
            source_ref.at[pl.ds(i * rows, rows)], target_ref.at[pl.ds(i * rows, rows)], semaphores.at[i]
        )
        for i in range(parts)
    ]
    for copy in copies:
        copy.start()
    for copy in copies:
        copy.wait()


def hold(weight):
    return pl.pallas_call(
        hold_kernel,
        in_specs=[pl.BlockSpec(memory_space=pl.ANY)],
        out_specs=pl.BlockSpec(memory_space=pltpu.VMEM),
        out_shape=pltpu.VMEM(weight.shape, weight.dtype),
        scratch_shapes=[pltpu.SemaphoreType.DMA((4,))],
        compiler_params=pltpu.CompilerParams(vmem_limit_bytes=54 * MIB),
        name="hold",
    )(weight)


def blocks_of(size, block):
    return [(first, min(block, size - first)) for first in range(0, size, block)]


def units_kernel(devices, experts, whole, scalars_ref, *refs):
    like_ref, other_ref, gain_ref, router_ref, routes_ref = refs[:5]
    gate_hbm, up_hbm, down_hbm, active_ref, weight_ref, odd_ref = refs[5:11]
    if whole:
        even_ref, normed_ref, gate_ref, up_ref, down_odd_ref, down_ref, semaphores = refs[11:]
    else:
        down_ref, normed_ref, gate_ref, up_ref, down_odd_ref, semaphores = refs[11:]
    spans = blocks_of(active_ref.shape[1], unit_block)
    count = len(spans)

    def fetch(n):
        first, size = spans[n]
        copies = [
            pltpu.make_async_copy(
                source.at[:, pl.ds(first, size)],
                target.at[n % 2, :, pl.ds(0, size)],
                semaphores.at[2 * n + i],
            )
            for i, (source, target) in enumerate(((gate_hbm, gate_ref), (up_hbm, up_ref)))
        ]
        for copy in copies:
            copy.start()
        return copies

    rank, expert = scalars_ref[0], scalars_ref[1]
    half, rows, columns = like_ref.shape
    model = devices * columns

    def fetch_down(n):
        parity, i = (1, n) if n < half else (0, n - half)
        first = pl.multiple_of((rank ^ (2 * i + parity)) * columns, columns)
        target = (down_odd_ref if parity else down_ref).at[i]
        copy = pltpu.make_async_copy(down_hbm.at[:, pl.ds(first, columns)], target, semaphores.at[2 * count + n])
        copy.start()
        return copy

    fetched, downs = [fetch(0)], []

    pieces = []
    for ref, parity in ((like_ref, 0), (other_ref, 1)):
        pieces += [(ref, i, rank ^ (2 * i + parity)) for i in range(devices // 2)]
    squares = jnp.zeros((rows, 1), f32)
    raw = jnp.zeros((rows, router_ref.shape[1]), f32)
    for ref, i, device in pieces:
        first = pl.multiple_of(device * columns, columns)
        value = ref[i].astype(f32)
        squares += jnp.sum(value * value, axis=1, keepdims=True)
        raw += jnp.dot(ref[i], router_ref[pl.ds(first, columns), :], preferred_element_type=f32)
    inverse = lax.rsqrt(squares / model + norm_eps)
    for ref, i, device in pieces:
        first = pl.multiple_of(device * columns, columns)
        value = ref[i].astype(f32) * inverse * gain_ref[device]
        normed_ref[:, pl.ds(first, columns)] = value.astype(bf16)
    logits = raw * inverse
    routes = routes_ref[...]
    one, two = routes[:, 0:1], routes[:, 1:2]
    lane = lax.broadcasted_iota(jnp.int32, raw.shape, 1)
    lane = jnp.where(lane < experts, lane, lane - experts)
    own_logit = jnp.sum(jnp.where(lane == expert, logits, 0.0), axis=1, keepdims=True)
    other_logit = jnp.sum(jnp.where(lane == one + two - expert, logits, 0.0), axis=1, keepdims=True)
    named = (one == expert) | (two == expert)
    weight = jnp.where(named, 1.0 / (1.0 + jnp.exp(other_logit - own_logit)), 0.0)
    weight_ref[...] = jnp.broadcast_to(weight, weight_ref.shape)

    for n, (first, size) in enumerate(spans):
        if n + 1 < count:
            fetched.append(fetch(n + 1))
        downs += [fetch_down(m) for m in range(len(downs), 2 * half * (n + 1) // (count + 1))]
        for copy in fetched[n]:
            copy.wait()
        block = n % 2, slice(None), pl.ds(0, size)
        gate = jnp.dot(normed_ref[...], gate_ref[block], preferred_element_type=f32)
        up = jnp.dot(normed_ref[...], up_ref[block], preferred_element_type=f32)
        active_ref[:, pl.ds(first, size)] = (gate / (1.0 + jnp.exp(-gate)) * up).astype(bf16)
    downs += [fetch_down(m) for m in range(len(downs), 2 * half)]
    for i in range(half):
        downs[i].wait()
        total = jnp.dot(active_ref[...], down_odd_ref[i], preferred_element_type=f32)
        odd_ref[i] = (total * weight_ref[:, 0:1]).astype(bf16)
    for i in range(half):
        downs[half + i].wait()
        if whole:
            total = jnp.dot(active_ref[...], down_ref[i], preferred_element_type=f32)
            even_ref[i] = (total * weight_ref[:, 0:1]).astype(bf16)


def run_units(experts, whole, scalars, like, other, gain, router, routes, weights):
    half, rows, columns = like.shape
    model, units = weights[0].shape
    in_vmem = pl.BlockSpec(memory_space=pltpu.VMEM)
    in_hbm = pl.BlockSpec(memory_space=pl.ANY)
    out_shape = [jax.ShapeDtypeStruct((rows, units), bf16), jax.ShapeDtypeStruct((rows, 128), f32)]
    out_shape.append(jax.ShapeDtypeStruct((half, rows, columns), bf16))
    down_half = pltpu.VMEM((half, units, columns), bf16)
    out_shape.append(out_shape[-1] if whole else down_half)
    block = min(unit_block, units)
    return pl.pallas_call(
        functools.partial(units_kernel, 2 * half, experts, whole),
        in_specs=[pl.BlockSpec(memory_space=pltpu.SMEM)] + [in_vmem] * 5 + [in_hbm] * len(weights),
        out_specs=[in_vmem] * len(out_shape),
        out_shape=out_shape,
        scratch_shapes=[
            pltpu.VMEM((rows, model), bf16),
            pltpu.VMEM((2, model, block), bf16),
            pltpu.VMEM((2, model, block), bf16),
            down_half,
            *([down_half] if whole else []),
            pltpu.SemaphoreType.DMA((2 * len(blocks_of(units, block)) + 2 * half,)),
        ],
        compiler_params=pltpu.CompilerParams(vmem_limit_bytes=(48 if whole else 44) * MIB),
        cost_estimate=pl.CostEstimate(
            flops=4 * rows * model * units, bytes_accessed=6 * model * units, transcendentals=rows * units
        ),
        name="units",
    )(scalars, like, other, gain, router, routes, *weights)


def down_kernel(active_ref, weight_ref, down_ref, out_ref):
    for i in range(out_ref.shape[0]):
        total = jnp.dot(active_ref[...], down_ref[i], preferred_element_type=f32)
        out_ref[i] = (total * weight_ref[:, 0:1]).astype(bf16)


def run_down(active, weight, down):
    rows = active.shape[0]
    half, units, columns = down.shape
    in_vmem = pl.BlockSpec(memory_space=pltpu.VMEM)
    return pl.pallas_call(
        down_kernel,
        in_specs=[in_vmem] * 3,
        out_specs=in_vmem,
        out_shape=jax.ShapeDtypeStruct((half, rows, columns), bf16),
        compiler_params=pltpu.CompilerParams(vmem_limit_bytes=8 * MIB),
        cost_estimate=pl.CostEstimate(
            flops=2 * rows * down.size, bytes_accessed=2 * down.size, transcendentals=0
        ),
        name="down",
    )(active, weight, down)


def fence(*values):
    return lax.optimization_barrier(values)


def between_chips(piece, sums):
    devices = lax.axis_size("tp")
    near, spread = [piece], [None if sums is None else sums[0]]
    for i in range(1, devices // 2):
        if piece is None:
            spread.append(xor_swap(sums[i], "tp", 2 * i))
        elif sums is None:
            near.append(xor_swap(piece, "tp", 2 * i))
        else:
            both = xor_swap(jnp.concatenate([piece, sums[i]], axis=0), "tp", 2 * i)
            near.append(both[: piece.shape[0]])
            spread.append(both[piece.shape[0] :])
    return (None if piece is None else near), (None if sums is None else spread)


def core_sums(like, arrived):
    return [
        (like[i].astype(f32) + arrived[i].astype(f32)).astype(bf16) for i in range(like.shape[0])
    ]


def add_up(parts):
    total = parts[0].astype(f32)
    for x in parts[1:]:
        total += x.astype(f32)
    return total


def per_device(
    queries,
    key_new,
    value_new,
    cache_keys,
    cache_values,
    context_lengths,
    residual,
    out_weight,
    norm_gain,
    router,
    routes,
    gate_weight,
    up_weight,
    down_weight,
):
    devices = lax.axis_size("tp")
    planes = lax.axis_size("req")
    rank = lax.axis_index("tp")
    plane = lax.axis_index("req")
    heads, width = queries.shape[1], queries.shape[2]
    key_heads = cache_keys.shape[2]
    grouping = heads * devices // key_heads
    own_keys = max(1, heads // grouping)
    model = out_weight.shape[1]
    columns = model // devices

    cache = jnp.stack([cache_keys, cache_values]).transpose(0, 3, 1, 2, 4)

    def slab(device):
        return lax.dynamic_slice_in_dim(cache, device * heads // grouping, own_keys, 1)

    cached = [slab(rank)] + [xor_swap(slab(rank ^ j), "tp", j) for j in range(1, devices)]
    first_key = rank * heads // grouping
    kn = lax.dynamic_slice_in_dim(key_new, first_key, own_keys, 1).transpose(1, 0, 2)
    vn = lax.dynamic_slice_in_dim(value_new, first_key, own_keys, 1).transpose(1, 0, 2)
    q = queries.transpose(1, 0, 2)
    gain = norm_gain.astype(f32)
    routing = gain[:, None] * router.astype(f32)
    high = routing.astype(bf16)
    low = (routing - high.astype(f32)).astype(bf16)
    routing = jnp.concatenate([high, low], axis=1)
    routing = jnp.pad(routing, ((0, 0), (0, -routing.shape[1] % 128)))
    gain = gain.reshape(devices, 1, columns)
    scalars = jnp.stack([rank, plane]).astype(jnp.int32)
    cached, out_held, routing, gain, scalars, q, kn, vn = fence(
        cached, hold(out_weight), routing, gain, scalars, q, kn, vn
    )

    like, other = attend(
        context_lengths, scalars[:1], cached, q, kn, vn, out_held, width**-0.5
    )
    sums = core_sums(like, xor_swap(other, "tp", 1))
    sums, own_routes = fence(sums, routes)
    _, parts = between_chips(None, sums)
    chunk_routes = [own_routes] + [xor_swap(own_routes, "req", k) for k in range(1, planes)]
    parts, chunk_routes = fence(parts, chunk_routes)
    hidden = (residual.astype(f32) + add_up(parts)).astype(bf16)

    groups = [[0]] + [list(range(k, min(k + 2, planes))) for k in range(1, planes, 2)]
    half = devices // 2
    span = hidden.shape[0]
    weights = [gate_weight[0], up_weight[0], down_weight[0]]

    def joined(arrays, group):
        return arrays[group[0]] if len(group) == 1 else jnp.concatenate([arrays[k] for k in group], axis=0)

    def rows_of(near):
        rows = jnp.stack(near)
        return rows, xor_swap(rows, "tp", 1)

    near, _ = between_chips(hidden, None)
    pieces = {k: xor_swap(hidden, "req", k) for k in range(1, min(planes, 3))}
    near, pieces, own = fence(near, pieces, hidden)
    pieces |= {k: xor_swap(own, "req", k) for k in range(3, planes)}
    like, other = rows_of(near)
    sums, back = None, {}

    def send_back(at, parts):
        total = add_up(parts)
        for i, k in enumerate(groups[at]):
            part = total[i * span : (i + 1) * span]
            back[k] = xor_swap(part.astype(bf16), "req", k) if k else part

    for at, group in enumerate(groups):
        following = groups[at + 1] if at + 1 < len(groups) else None
        near, spread = between_chips(joined(pieces, following) if following else None, sums)
        active, weight, odd, down = run_units(
            planes, at == 0, scalars, like, other, gain, routing, joined(chunk_routes, group), weights
        )
        active, weight, odd, down = fence(active, weight, odd, down)
        if following:
            near, spread, pieces, active = fence(near, spread, pieces, active)
            like, other = rows_of(near)
            if spread:
                send_back(at - 1, spread)
        arrived = xor_swap(odd, "tp", 1)
        even = run_down(active, weight, down) if at > 0 else down
        if following:
            even, arrived, other, pieces = fence(even, arrived, other, pieces)
        else:
            even, arrived = fence(even, arrived)
            if spread:
                send_back(at - 1, spread)
        sums = core_sums(even, arrived)
    _, spread = between_chips(None, sums)
    send_back(len(groups) - 1, spread)
    total = hidden.astype(f32)
    for k in range(planes):
        total += back[k].astype(f32)
    return total.astype(bf16)


def solution(mesh):
    placed = (
        P("req", "tp", None),
        P("req", None, None),
        P("req", None, None),
        P("req", "tp", None, None),
        P("req", "tp", None, None),
        P("req"),
        P("req", "tp"),
        P("tp", None),
        P(),
        P(),
        P("req", None),
        P("req", None, "tp"),
        P("req", None, "tp"),
        P("req", "tp", None),
    )
    return jax.shard_map(
        per_device, mesh=mesh, in_specs=placed, out_specs=P("req", "tp"), check_vma=False
    )
```

```python
import functools
import jax
import jax.numpy as jnp
from jax import lax
from jax.experimental import pallas as pl
from jax.experimental.pallas import tpu as pltpu
from jax.sharding import PartitionSpec as P

norm_eps = 1e-05
masked_score = -1e30
bf16 = jnp.bfloat16
f32 = jnp.float32
MIB = 1 << 20
unit_block = 512


def xor_swap(x, axis, mask):
    size = lax.axis_size(axis)
    return lax.ppermute(x, axis, [(i, i ^ mask) for i in range(size)])


def attend_kernel(devices, groups, scaling, lengths_ref, rank_ref, *refs):
    pieces, (q_ref, kn_ref, vn_ref, ow_ref, like_ref, other_ref) = refs[:devices], refs[devices:]
    rank = rank_ref[0]
    length = lengths_ref[pl.program_id(0)]
    key_heads, new_rows, width = kn_ref.shape
    span = pieces[0].shape[3]
    columns = like_ref.shape[2]
    cached = devices * span
    column = lax.broadcasted_iota(jnp.int32, (new_rows, cached), 1)
    place = (rank ^ (column // span)) * span + column % span
    far_bias = jnp.where(place < length, 0.0, masked_score)
    row = lax.broadcasted_iota(jnp.int32, (new_rows, new_rows), 0)
    step = lax.broadcasted_iota(jnp.int32, (new_rows, new_rows), 1)
    near_bias = jnp.where(step <= row, 0.0, masked_score)
    bias = jnp.concatenate([far_bias, near_bias], axis=1)
    outs = []
    for head in range(key_heads):
        keys = jnp.concatenate([p[0, head, 0] for p in pieces] + [kn_ref[head]], axis=0)
        values = jnp.concatenate([p[1, head, 0] for p in pieces] + [vn_ref[head]], axis=0)
        for g in range(groups):
            q = q_ref[head * groups + g]
            scores = (
                lax.dot_general(q, keys, (((1,), (1,)), ((), ())), preferred_element_type=f32)
                * scaling
            )
            scores = jnp.where(bias < 0.0, masked_score, scores)
            highest = jnp.max(scores, axis=1, keepdims=True)
            weights = jnp.exp(scores - highest)
            total = jnp.sum(weights, axis=1, keepdims=True)
            mixed = jnp.dot(weights.astype(bf16), values, preferred_element_type=f32)
            outs.append((mixed / total).astype(bf16))
    attention = jnp.concatenate(outs, axis=1)
    for target, parity in ((like_ref, 0), (other_ref, 1)):
        for i in range(devices // 2):
            first = pl.multiple_of((rank ^ (2 * i + parity)) * columns, columns)
            term = jnp.dot(attention, ow_ref[:, pl.ds(first, columns)], preferred_element_type=f32)
            target[i] = term.astype(bf16)


def attend(lengths, rank, cached, q, kn, vn, out_weight, scaling):
    devices = len(cached)
    _, key_heads, requests, span, width = cached[0].shape
    heads, rows, _ = q.shape
    new_rows = rows // requests
    model = out_weight.shape[1]
    columns = model // devices
    cached_spec = pl.BlockSpec((2, key_heads, 1, span, width), lambda r, *_: (0, 0, r, 0, 0))
    near_spec = pl.BlockSpec((key_heads, new_rows, width), lambda r, *_: (0, r, 0))
    out_spec = pl.BlockSpec((devices // 2, new_rows, columns), lambda r, *_: (0, r, 0))
    out_type = jax.ShapeDtypeStruct((devices // 2, rows, columns), bf16)
    flops = 4 * rows * heads * width * (devices * span + new_rows) + 2 * rows * heads * width * model
    return pl.pallas_call(
        functools.partial(attend_kernel, devices, heads // key_heads, scaling),
        grid_spec=pltpu.PrefetchScalarGridSpec(
            num_scalar_prefetch=2,
            grid=(requests,),
            in_specs=[cached_spec] * devices
            + [
                pl.BlockSpec((heads, new_rows, width), lambda r, *_: (0, r, 0)),
                near_spec,
                near_spec,
                pl.BlockSpec(memory_space=pltpu.VMEM),
            ],
            out_specs=[out_spec, out_spec],
        ),
        out_shape=[out_type, out_type],
        compiler_params=pltpu.CompilerParams(vmem_limit_bytes=24 * MIB),
        cost_estimate=pl.CostEstimate(
            flops=flops, bytes_accessed=8 * MIB, transcendentals=rows * heads * devices * span
        ),
        name="attend",
    )(lengths, rank, *cached, q, kn, vn, out_weight)


def hold_kernel(source_ref, target_ref, semaphores):
    parts = semaphores.shape[0]
    rows = source_ref.shape[0] // parts
    copies = [
        pltpu.make_async_copy(
            source_ref.at[pl.ds(i * rows, rows)], target_ref.at[pl.ds(i * rows, rows)], semaphores.at[i]
        )
        for i in range(parts)
    ]
    for copy in copies:
        copy.start()
    for copy in copies:
        copy.wait()


def hold(weight):
    return pl.pallas_call(
        hold_kernel,
        in_specs=[pl.BlockSpec(memory_space=pl.ANY)],
        out_specs=pl.BlockSpec(memory_space=pltpu.VMEM),
        out_shape=pltpu.VMEM(weight.shape, weight.dtype),
        scratch_shapes=[pltpu.SemaphoreType.DMA((4,))],
        compiler_params=pltpu.CompilerParams(vmem_limit_bytes=54 * MIB),
        name="hold",
    )(weight)


def blocks_of(size, block):
    return [(first, min(block, size - first)) for first in range(0, size, block)]


def units_kernel(devices, experts, whole, scalars_ref, *refs):
    like_ref, other_ref, gain_ref, router_ref, routes_ref = refs[:5]
    gate_hbm, up_hbm, down_hbm, active_ref, weight_ref, odd_ref = refs[5:11]
    if whole:
        even_ref, normed_ref, gate_ref, up_ref, down_odd_ref, down_ref, semaphores = refs[11:]
    else:
        down_ref, normed_ref, gate_ref, up_ref, down_odd_ref, semaphores = refs[11:]
    spans = blocks_of(active_ref.shape[1], unit_block)
    count = len(spans)

    def fetch(n):
        first, size = spans[n]
        copies = [
            pltpu.make_async_copy(
                source.at[:, pl.ds(first, size)],
                target.at[n % 2, :, pl.ds(0, size)],
                semaphores.at[2 * n + i],
            )
            for i, (source, target) in enumerate(((gate_hbm, gate_ref), (up_hbm, up_ref)))
        ]
        for copy in copies:
            copy.start()
        return copies

    rank, expert = scalars_ref[0], scalars_ref[1]
    half, rows, columns = like_ref.shape
    model = devices * columns

    def fetch_down(n):
        parity, i = (1, n) if n < half else (0, n - half)
        first = pl.multiple_of((rank ^ (2 * i + parity)) * columns, columns)
        target = (down_odd_ref if parity else down_ref).at[i]
        copy = pltpu.make_async_copy(down_hbm.at[:, pl.ds(first, columns)], target, semaphores.at[2 * count + n])
        copy.start()
        return copy

    fetched, downs = [fetch(0)], []

    pieces = []
    for ref, parity in ((like_ref, 0), (other_ref, 1)):
        pieces += [(ref, i, rank ^ (2 * i + parity)) for i in range(devices // 2)]
    squares = jnp.zeros((rows, 1), f32)
    raw = jnp.zeros((rows, router_ref.shape[1]), f32)
    for ref, i, device in pieces:
        first = pl.multiple_of(device * columns, columns)
        value = ref[i].astype(f32)
        squares += jnp.sum(value * value, axis=1, keepdims=True)
        raw += jnp.dot(ref[i], router_ref[pl.ds(first, columns), :], preferred_element_type=f32)
    inverse = lax.rsqrt(squares / model + norm_eps)
    for ref, i, device in pieces:
        first = pl.multiple_of(device * columns, columns)
        value = ref[i].astype(f32) * inverse * gain_ref[device]
        normed_ref[:, pl.ds(first, columns)] = value.astype(bf16)
    logits = raw * inverse
    routes = routes_ref[...]
    one, two = routes[:, 0:1], routes[:, 1:2]
    lane = lax.broadcasted_iota(jnp.int32, raw.shape, 1)
    lane = jnp.where(lane < experts, lane, lane - experts)
    own_logit = jnp.sum(jnp.where(lane == expert, logits, 0.0), axis=1, keepdims=True)
    other_logit = jnp.sum(jnp.where(lane == one + two - expert, logits, 0.0), axis=1, keepdims=True)
    named = (one == expert) | (two == expert)
    weight = jnp.where(named, 1.0 / (1.0 + jnp.exp(other_logit - own_logit)), 0.0)
    weight_ref[...] = jnp.broadcast_to(weight, weight_ref.shape)

    for n, (first, size) in enumerate(spans):
        if n + 1 < count:
            fetched.append(fetch(n + 1))
        downs += [fetch_down(m) for m in range(len(downs), 2 * half * (n + 1) // (count + 1))]
        for copy in fetched[n]:
            copy.wait()
        block = n % 2, slice(None), pl.ds(0, size)
        gate = jnp.dot(normed_ref[...], gate_ref[block], preferred_element_type=f32)
        up = jnp.dot(normed_ref[...], up_ref[block], preferred_element_type=f32)
        active_ref[:, pl.ds(first, size)] = (gate / (1.0 + jnp.exp(-gate)) * up).astype(bf16)
    downs += [fetch_down(m) for m in range(len(downs), 2 * half)]
    for i in range(half):
        downs[i].wait()
        total = jnp.dot(active_ref[...], down_odd_ref[i], preferred_element_type=f32)
        odd_ref[i] = (total * weight_ref[:, 0:1]).astype(bf16)
    for i in range(half):
        downs[half + i].wait()
        if whole:
            total = jnp.dot(active_ref[...], down_ref[i], preferred_element_type=f32)
            even_ref[i] = (total * weight_ref[:, 0:1]).astype(bf16)


def run_units(experts, whole, scalars, like, other, gain, router, routes, weights):
    half, rows, columns = like.shape
    model, units = weights[0].shape
    in_vmem = pl.BlockSpec(memory_space=pltpu.VMEM)
    in_hbm = pl.BlockSpec(memory_space=pl.ANY)
    out_shape = [jax.ShapeDtypeStruct((rows, units), bf16), jax.ShapeDtypeStruct((rows, 128), f32)]
    out_shape.append(jax.ShapeDtypeStruct((half, rows, columns), bf16))
    down_half = pltpu.VMEM((half, units, columns), bf16)
    out_shape.append(out_shape[-1] if whole else down_half)
    block = min(unit_block, units)
    return pl.pallas_call(
        functools.partial(units_kernel, 2 * half, experts, whole),
        in_specs=[pl.BlockSpec(memory_space=pltpu.SMEM)] + [in_vmem] * 5 + [in_hbm] * len(weights),
        out_specs=[in_vmem] * len(out_shape),
        out_shape=out_shape,
        scratch_shapes=[
            pltpu.VMEM((rows, model), bf16),
            pltpu.VMEM((2, model, block), bf16),
            pltpu.VMEM((2, model, block), bf16),
            down_half,
            *([down_half] if whole else []),
            pltpu.SemaphoreType.DMA((2 * len(blocks_of(units, block)) + 2 * half,)),
        ],
        compiler_params=pltpu.CompilerParams(vmem_limit_bytes=(48 if whole else 44) * MIB),
        cost_estimate=pl.CostEstimate(
            flops=4 * rows * model * units, bytes_accessed=6 * model * units, transcendentals=rows * units
        ),
        name="units",
    )(scalars, like, other, gain, router, routes, *weights)


def down_kernel(active_ref, weight_ref, down_ref, out_ref):
    for i in range(out_ref.shape[0]):
        total = jnp.dot(active_ref[...], down_ref[i], preferred_element_type=f32)
        out_ref[i] = (total * weight_ref[:, 0:1]).astype(bf16)


def run_down(active, weight, down):
    rows = active.shape[0]
    half, units, columns = down.shape
    in_vmem = pl.BlockSpec(memory_space=pltpu.VMEM)
    return pl.pallas_call(
        down_kernel,
        in_specs=[in_vmem] * 3,
        out_specs=in_vmem,
        out_shape=jax.ShapeDtypeStruct((half, rows, columns), bf16),
        compiler_params=pltpu.CompilerParams(vmem_limit_bytes=8 * MIB),
        cost_estimate=pl.CostEstimate(
            flops=2 * rows * down.size, bytes_accessed=2 * down.size, transcendentals=0
        ),
        name="down",
    )(active, weight, down)


def fence(*values):
    return lax.optimization_barrier(values)


def between_chips(piece, sums):
    devices = lax.axis_size("tp")
    near, spread = [piece], [None if sums is None else sums[0]]
    for i in range(1, devices // 2):
        if piece is None:
            spread.append(xor_swap(sums[i], "tp", 2 * i))
        elif sums is None:
            near.append(xor_swap(piece, "tp", 2 * i))
        else:
            both = xor_swap(jnp.concatenate([piece, sums[i]], axis=0), "tp", 2 * i)
            near.append(both[: piece.shape[0]])
            spread.append(both[piece.shape[0] :])
    return (None if piece is None else near), (None if sums is None else spread)


def core_sums(like, arrived):
    return [
        (like[i].astype(f32) + arrived[i].astype(f32)).astype(bf16) for i in range(like.shape[0])
    ]


def add_up(parts):
    total = parts[0].astype(f32)
    for x in parts[1:]:
        total += x.astype(f32)
    return total


def per_device(
    queries,
    key_new,
    value_new,
    cache_keys,
    cache_values,
    context_lengths,
    residual,
    out_weight,
    norm_gain,
    router,
    routes,
    gate_weight,
    up_weight,
    down_weight,
):
    devices = lax.axis_size("tp")
    planes = lax.axis_size("req")
    rank = lax.axis_index("tp")
    plane = lax.axis_index("req")
    heads, width = queries.shape[1], queries.shape[2]
    key_heads = cache_keys.shape[2]
    grouping = heads * devices // key_heads
    own_keys = max(1, heads // grouping)
    model = out_weight.shape[1]
    columns = model // devices

    cache = jnp.stack([cache_keys, cache_values]).transpose(0, 3, 1, 2, 4)

    def slab(device):
        return lax.dynamic_slice_in_dim(cache, device * heads // grouping, own_keys, 1)

    cached = [slab(rank)] + [xor_swap(slab(rank ^ j), "tp", j) for j in range(1, devices)]
    first_key = rank * heads // grouping
    kn = lax.dynamic_slice_in_dim(key_new, first_key, own_keys, 1).transpose(1, 0, 2)
    vn = lax.dynamic_slice_in_dim(value_new, first_key, own_keys, 1).transpose(1, 0, 2)
    q = queries.transpose(1, 0, 2)
    gain = norm_gain.astype(f32)
    routing = gain[:, None] * router.astype(f32)
    high = routing.astype(bf16)
    low = (routing - high.astype(f32)).astype(bf16)
    routing = jnp.concatenate([high, low], axis=1)
    routing = jnp.pad(routing, ((0, 0), (0, -routing.shape[1] % 128)))
    gain = gain.reshape(devices, 1, columns)
    scalars = jnp.stack([rank, plane]).astype(jnp.int32)
    cached, out_held, routing, gain, scalars, q, kn, vn = fence(
        cached, hold(out_weight), routing, gain, scalars, q, kn, vn
    )

    like, other = attend(
        context_lengths, scalars[:1], cached, q, kn, vn, out_held, width**-0.5
    )
    sums = core_sums(like, xor_swap(other, "tp", 1))
    sums, own_routes = fence(sums, routes)
    _, parts = between_chips(None, sums)
    chunk_routes = [own_routes] + [xor_swap(own_routes, "req", k) for k in range(1, planes)]
    parts, chunk_routes = fence(parts, chunk_routes)
    hidden = (residual.astype(f32) + add_up(parts)).astype(bf16)

    groups = [[0]] + [list(range(k, min(k + 2, planes))) for k in range(1, planes, 2)]
    half = devices // 2
    span = hidden.shape[0]
    weights = [gate_weight[0], up_weight[0], down_weight[0]]

    def joined(arrays, group):
        return arrays[group[0]] if len(group) == 1 else jnp.concatenate([arrays[k] for k in group], axis=0)

    def rows_of(near):
        rows = jnp.stack(near)
        return rows, xor_swap(rows, "tp", 1)

    near, _ = between_chips(hidden, None)
    pieces = {k: xor_swap(hidden, "req", k) for k in range(1, min(planes, 3))}
    near, pieces, own = fence(near, pieces, hidden)
    pieces |= {k: xor_swap(own, "req", k) for k in range(3, planes)}
    like, other = rows_of(near)
    sums, back = None, {}

    def send_back(at, parts):
        total = add_up(parts)
        for i, k in enumerate(groups[at]):
            part = total[i * span : (i + 1) * span]
            back[k] = xor_swap(part.astype(bf16), "req", k) if k else part

    for at, group in enumerate(groups):
        following = groups[at + 1] if at + 1 < len(groups) else None
        near, spread = between_chips(joined(pieces, following) if following else None, sums)
        active, weight, odd, down = run_units(
            planes, at == 0, scalars, like, other, gain, routing, joined(chunk_routes, group), weights
        )
        near, spread, pieces, active, weight, odd, down = fence(
            near, spread, pieces, active, weight, odd, down
        )
        if following:
            like, other = rows_of(near)
        if spread:
            send_back(at - 1, spread)
        arrived = xor_swap(odd, "tp", 1)
        even = run_down(active, weight, down) if at > 0 else down
        even, arrived, other, pieces = fence(even, arrived, other, pieces)
        sums = core_sums(even, arrived)
    _, spread = between_chips(None, sums)
    send_back(len(groups) - 1, spread)
    total = hidden.astype(f32)
    for k in range(planes):
        total += back[k].astype(f32)
    return total.astype(bf16)


def solution(mesh):
    placed = (
        P("req", "tp", None),
        P("req", None, None),
        P("req", None, None),
        P("req", "tp", None, None),
        P("req", "tp", None, None),
        P("req"),
        P("req", "tp"),
        P("tp", None),
        P(),
        P(),
        P("req", None),
        P("req", None, "tp"),
        P("req", None, "tp"),
        P("req", "tp", None),
    )
    return jax.shard_map(
        per_device, mesh=mesh, in_specs=placed, out_specs=P("req", "tp"), check_vma=False
    )
```
